32 devices in a mesh: strip: 4 (over y, core), tensor: 8 (over z, x).
Axes of the slice: x: 2, y: 2, z: 4, core: 2. Of those that a mesh axis runs over, the one named last changes fastest.
Arguments:
- conv_out: bfloat16 [32, 128, 1536], P('strip', 'tensor'), may hold values from -425 to 425
- out_grad: bfloat16 [32, 128, 1536], P('strip', 'tensor'), may hold values from -6 to 6
- layer_norm_gain: float32 [1536], replicated, may hold values from 0.5 to 2
- layer_norm_bias: float32 [1536], replicated, may hold values from -3 to 3
- w_in: bfloat16 [1536, 6144], P('strip', 'tensor'), may hold values from -0.15625 to 0.15625
- b_in: float32 [6144], P('tensor'), may hold values from -3 to 3
- w_out: bfloat16 [6144, 1536], P('tensor', 'strip'), may hold values from -0.078125 to 0.078125
- layer_scale: float32 [1536], replicated, may hold values from 0.25 to 2
- dw_kernel: float32 [7, 7, 1536], replicated, may hold values from -0.875 to 0.875
Outputs:
- grad_input: bfloat16 [32, 128, 1536], P('strip', 'tensor')
- grad_w_in: float32 [1536, 6144], P('strip', 'tensor')
- grad_w_out: float32 [6144, 1536], P('tensor', 'strip')
The draws below stay inside these ranges and needn't reach their ends.
All inputs are finite; a program needn't handle non-finite values.
Results may differ from the reference program's by a relative error of at most 0.0063.
Values may be sent and summed in bfloat16 or wider, within the bound.
A program may use at most 128 MiB of HBM per device.

```python
import math
import jax
import jax.numpy as jnp
from jax import lax

C = 1536
HID = 6144
KSIZE = 7
IMG_ROWS = 32
IMG_COLS = 128


def draw_conv_out(key, part):
    keys = jax.random.split(key, 4)
    shape = (IMG_ROWS, IMG_COLS, C)
    base = jnp.clip(jax.random.normal(keys[0], shape, jnp.float32), -4.0, 4.0)
    row_scale = jnp.exp(jax.random.uniform(keys[1], (IMG_ROWS, IMG_COLS, 1), jnp.float32, 0.0, math.log(10.0)))
    col_scale = jnp.exp(jax.random.uniform(keys[2], (1, 1, C), jnp.float32, 0.0, math.log(10.0)))
    offset = jax.random.uniform(keys[3], (1, 1, C), jnp.float32, -2.0, 2.0)
    return (row_scale * (base * col_scale + offset)).astype(jnp.bfloat16)


def with_spikes(result, stream_key, source, target, blocks, factor):
    owner, partner = [(jnp.arange(result.shape[position]) // (result.shape[position] // blocks)).reshape([-1 if axis == position else 1 for axis in range(result.ndim)]) for position in (source, target)]
    chosen = jax.random.permutation(stream_key, blocks)[partner]
    strong = (owner == chosen) | (owner == (partner + blocks // 2) % blocks)
    return jnp.where(strong, factor * result, result)


def block_levels(rng, dims, cuts, least, high):
    gain = 1.0
    for axis_at, blocks in cuts:
        heights = jax.random.uniform(jax.random.fold_in(jax.random.fold_in(rng, 6), axis_at), (blocks,), jnp.float32, least / len(cuts), high / len(cuts))
        gain = gain * jnp.repeat(jnp.exp(heights), dims[axis_at] // blocks).reshape((-1,) + (1,) * (len(dims) - 1 - axis_at))
    return gain


def noise(stream_key, dims, deviation, limit, cuts=(), dtype=jnp.bfloat16):
    values = jax.random.normal(stream_key, dims, jnp.float32) * deviation
    if len(cuts) > 0:
        values = block_levels(stream_key, dims, cuts, -0.22, 0.18) * values
    return jnp.clip(values, min=-limit, max=limit).astype(dtype)


def bell_draw_with(own_key, dims, scale, limit, cuts, heavy, kind=jnp.bfloat16):
    array = scale * jax.random.normal(own_key, dims, jnp.float32)
    if cuts:
        array = array * block_levels(own_key, dims, cuts, -0.22, 0.18)
    return jnp.clip(with_spikes(array, jax.random.fold_in(own_key, 3), *heavy), -limit, limit).astype(kind)


def setup_inputs(seed: int = 0) -> dict:
    streams_of = jax.random.split(jax.random.key(seed), 10)
    conv_out = draw_conv_out(jax.random.fold_in(streams_of[9], 71), 0)
    out_grad = bell_draw_with(streams_of[1], (IMG_ROWS, IMG_COLS, C), 1.0, 6.0, ((0, 4), (1, 8)), (0, 2, 4, 2.0))
    layer_norm_gain = jnp.clip(jnp.exp(jax.random.uniform(streams_of[2], (C,), jnp.float32, math.log(0.5), math.log(2.0))), 0.5, 2.0)
    layer_norm_bias = noise(streams_of[3], (C,), 0.5, 3.0, (), jnp.float32)
    w_in = noise(streams_of[4], (C, HID), C ** -0.5, 0.15625, ((0, 4), (1, 8)))
    b_in = noise(streams_of[5], (HID,), 0.5, 3.0, ((0, 8),), jnp.float32)
    w_out = noise(streams_of[6], (HID, C), HID ** -0.5, 0.078125, ((0, 8), (1, 4)))
    layer_scale = jnp.clip(jnp.exp(jax.random.uniform(streams_of[7], (C,), jnp.float32, math.log(0.25), math.log(2.0))), 0.25, 2.0)
    dw_kernel = noise(streams_of[8], (KSIZE, KSIZE, C), (KSIZE * KSIZE) ** -0.5, 0.875, (), jnp.float32)
    return {"conv_out": conv_out, "out_grad": out_grad, "layer_norm_gain": layer_norm_gain, "layer_norm_bias": layer_norm_bias, "w_in": w_in, "b_in": b_in, "w_out": w_out, "layer_scale": layer_scale, "dw_kernel": dw_kernel}


ln_eps = 1e-06
root_half = 0.7071067811865476
density_norm = 0.3989422804014327

def gelu_value(value):
    return 0.5 * value * (1.0 + lax.erf(value * root_half))

def gelu_slope(value):
    return 0.5 * (1.0 + lax.erf(value * root_half)) + value * jnp.exp(-0.5 * value * value) * density_norm

def apply_layer_norm(flattened_rows):
    centre = lax.optimization_barrier(jnp.mean(flattened_rows, axis=-1, keepdims=True))
    centred = flattened_rows - centre
    spread = lax.optimization_barrier(jnp.mean(centred * centred, axis=-1, keepdims=True))
    inverse_deviation = lax.rsqrt(spread + ln_eps)
    return (centred * inverse_deviation, inverse_deviation)

def layer_norm_backward(normed_gradient, centred_input, inverse_deviation, layer_norm_gain):
    gain_scaled = normed_gradient * layer_norm_gain
    first_moment = lax.optimization_barrier(jnp.mean(gain_scaled, axis=-1, keepdims=True))
    second_moment = lax.optimization_barrier(jnp.mean(gain_scaled * centred_input, axis=-1, keepdims=True))
    return inverse_deviation * (gain_scaled - first_moment - centred_input * second_moment)

def transpose_conv(padded, dw_kernel, image_height, image_breadth):
    taps = dw_kernel.shape[0]
    total = jnp.zeros((image_height, image_breadth, padded.shape[2]), jnp.float32)
    for row_tap in range(taps):
        for col_tap in range(taps):
            start_row = taps - 1 - row_tap
            start_col = taps - 1 - col_tap
            total = total + dw_kernel[row_tap, col_tap] * padded[start_row:start_row + image_height, start_col:start_col + image_breadth]
    return total

def reference(conv_out, out_grad, layer_norm_gain, layer_norm_bias, w_in, b_in, w_out, layer_scale, dw_kernel):
    image_height, image_breadth, channel_count = conv_out.shape
    count = image_height * image_breadth
    hidden = w_in.shape[1]
    flattened_rows = conv_out.astype(jnp.float32).reshape(count, channel_count)
    centred_input, inverse_deviation = apply_layer_norm(flattened_rows)
    normed_output = (centred_input * layer_norm_gain + layer_norm_bias).astype(jnp.bfloat16)
    upstream = out_grad.astype(jnp.float32).reshape(count, channel_count)
    scaled_grad = (upstream * layer_scale).astype(jnp.bfloat16)
    block = math.gcd(count, 4096)

    def advance(carry, pieces):
        grad_in, grad_out = carry
        normed_blk, scaled_blk = pieces
        pre_act = jnp.dot(normed_blk, w_in, preferred_element_type=jnp.float32) + b_in
        hidden_act = gelu_value(pre_act).astype(jnp.bfloat16)
        back_act = lax.dot_general(scaled_blk, w_out, (((1,), (1,)), ((), ())), preferred_element_type=jnp.float32)
        back_pre = (back_act * gelu_slope(pre_act)).astype(jnp.bfloat16)
        grad_in = grad_in + lax.dot_general(normed_blk, back_pre, (((0,), (0,)), ((), ())), preferred_element_type=jnp.float32)
        grad_out = grad_out + lax.dot_general(hidden_act, scaled_blk, (((0,), (0,)), ((), ())), preferred_element_type=jnp.float32)
        normed_gradient = lax.dot_general(back_pre, w_in, (((1,), (1,)), ((), ())), preferred_element_type=jnp.float32)
        return ((grad_in, grad_out), normed_gradient)
    start = (jnp.zeros((channel_count, hidden), jnp.float32), jnp.zeros((hidden, channel_count), jnp.float32))
    (grad_in, grad_out), normed_gradient = lax.scan(advance, start, (normed_output.reshape(-1, block, channel_count), scaled_grad.reshape(-1, block, channel_count)))
    normed_gradient = normed_gradient.reshape(count, channel_count)
    factor = 1.0 / math.sqrt(count)
    convolution_gradient = layer_norm_backward(normed_gradient, centred_input, inverse_deviation, layer_norm_gain).astype(jnp.bfloat16).reshape(image_height, image_breadth, channel_count)
    margin = dw_kernel.shape[0] // 2
    padded = jnp.pad(convolution_gradient.astype(jnp.float32), ((margin, margin), (margin, margin), (0, 0)))
    grad_input = (upstream.reshape(image_height, image_breadth, channel_count) + transpose_conv(padded, dw_kernel, image_height, image_breadth)).astype(jnp.bfloat16)
    return (grad_input, grad_in * factor, grad_out * factor)
```

```python
import functools
import math

import jax
import jax.numpy as jnp
from jax import lax
from jax.experimental import pallas as pl
from jax.experimental.pallas import tpu as pltpu
from jax.sharding import PartitionSpec as P

ln_eps = 1e-06
root_half = 0.7071067811865476
density_norm = 0.3989422804014327
MESH = pl.DeviceIdType.MESH
F32 = jnp.float32
BF16 = jnp.bfloat16


def with_halo(block, sides, width):
    for axis, dim in sides:
        count = lax.axis_size(axis)
        forward = [(i, i + 1) for i in range(count - 1)]
        backward = [(target, source) for source, target in forward]
        low = lax.ppermute(
            lax.slice_in_dim(block, block.shape[dim] - width, None, axis=dim), axis, forward
        )
        high = lax.ppermute(lax.slice_in_dim(block, 0, width, axis=dim), axis, backward)
        block = jnp.concatenate([low, block, high], axis=dim)
    return block


def gelu_value(value):
    return 0.5 * value * (1.0 + lax.erf(value * root_half))


def gelu_slope(value):
    return (
        0.5 * (1.0 + lax.erf(value * root_half))
        + value * jnp.exp(-0.5 * value * value) * density_norm
    )


def apply_layer_norm(flattened_rows):
    centre = jnp.mean(flattened_rows, axis=-1, keepdims=True)
    centred = flattened_rows - centre
    spread = jnp.mean(centred * centred, axis=-1, keepdims=True)
    inverse_deviation = lax.rsqrt(spread + ln_eps)
    return (centred * inverse_deviation, inverse_deviation)


def layer_norm_backward(normed_gradient, centred_input, inverse_deviation, layer_norm_gain):
    gain_scaled = normed_gradient * layer_norm_gain
    first_moment = jnp.mean(gain_scaled, axis=-1, keepdims=True)
    second_moment = jnp.mean(gain_scaled * centred_input, axis=-1, keepdims=True)
    return inverse_deviation * (gain_scaled - first_moment - centred_input * second_moment)


def transpose_conv(padded, dw_kernel, image_height, image_breadth):
    taps = dw_kernel.shape[0]
    total = jnp.zeros((image_height, image_breadth, padded.shape[2]), jnp.float32)
    for row_tap in range(taps):
        for col_tap in range(taps):
            start_row = taps - 1 - row_tap
            start_col = taps - 1 - col_tap
            total = (
                total
                + dw_kernel[row_tap, col_tap]
                * padded[
                    start_row : start_row + image_height, start_col : start_col + image_breadth
                ]
            )
    return total


def nt(a, b):
    return lax.dot_general(a, b, (((1,), (1,)), ((), ())), preferred_element_type=F32)


def tn(a, b):
    return lax.dot_general(a, b, (((0,), (0,)), ((), ())), preferred_element_type=F32)


def block_kernel(
    factor,
    conv_ref, grad_ref, gain_ref, bias_ref, win_ref, bin_ref, wout_ref, scale_ref,
    gconv_ref, gin_ref, gout_ref,
    tok, win, wout, hid, bp, acc_in, acc_out, xhat, inv,
    gown, gsend, gxrecv, zsend, zrecv, total,
    csend_in, csend_out, crecv_in, crecv_out, ysend_in, ysend_out, yrecv_in, yrecv_out,
    wy_s, wy_r, wc_s, wc_r, az_s, az_r, ax_s, ax_r, gx_s, gx_r, gz_s, gz_r,
    cs, cr, ys, yr,
):
    count, channels = conv_ref.shape
    shard, wide = win_ref.shape
    strip = lax.axis_index("strip")
    tensor = lax.axis_index("tensor")
    y, core = strip // 2, strip % 2
    z, x = tensor // 2, tensor % 2
    up = z // 2
    zm = z * (1 - up) + (3 - z) * up
    ypeer = 2 * (1 - y) + core
    cpeer = 2 * y + 1 - core
    xpeer = 2 * z + 1 - x

    def unmirror(m):
        return m * (1 - up) + (3 - m) * up

    def order(i):
        hi = i // 2
        return unmirror(hi * i + (1 - hi) * (i + zm - 2 * i * zm))

    def copy(src, dst, s, r, **where):
        return pltpu.make_async_remote_copy(
            src_ref=src, dst_ref=dst, send_sem=s, recv_sem=r, device_id=where, device_id_type=MESH
        )

    def rows(b, xx):
        return pl.ds(pl.multiple_of((2 * b + xx) * count, count), count)

    barrier = pltpu.get_barrier_semaphore()
    pl.semaphore_signal(barrier, inc=1, device_id={"strip": ypeer}, device_id_type=MESH)
    pl.semaphore_signal(barrier, inc=1, device_id={"strip": cpeer}, device_id_type=MESH)
    pl.semaphore_signal(barrier, inc=1, device_id={"tensor": xpeer}, device_id_type=MESH)
    for d in range(1, 4):
        other = 2 * ((z + d) % 4) + x
        pl.semaphore_signal(barrier, inc=1, device_id={"tensor": other}, device_id_type=MESH)

    def win_rows(s):
        return win.at[pl.ds(pl.multiple_of(s * shard, shard), shard)]

    def wout_cols(s):
        return wout.at[:, pl.ds(pl.multiple_of(s * shard, 128), shard)]

    def az_copy(k, h, b, dest):
        piece = tok.at[h, rows(b, x)]
        return copy(piece, piece, az_s.at[k, h], az_r.at[b, h], tensor=2 * dest + x)

    def ax_copy(h, b, xx):
        piece = tok.at[h, rows(b, xx)]
        return copy(piece, piece, ax_s.at[b, h], ax_r.at[b, h], tensor=xpeer)

    def own_sends(h):
        az_copy(0, h, z, unmirror(zm + 1)).start()

        @pl.when(zm == 1)
        def _():
            az_copy(1, h, z, unmirror(0)).start()

        ax_copy(h, z, x).start()

    wy = [
        copy(win_ref, win_rows(strip), wy_s.at[0], wy_r.at[0], strip=ypeer),
        copy(wout_ref, wout_cols(strip), wy_s.at[1], wy_r.at[1], strip=ypeer),
    ]
    wc = [
        copy(win_ref, win_rows(strip), wc_s.at[0], wc_r.at[0], strip=cpeer),
        copy(wout_ref, wout_cols(strip), wc_s.at[1], wc_r.at[1], strip=cpeer),
        copy(win_rows(ypeer), win_rows(ypeer), wc_s.at[2], wc_r.at[2], strip=cpeer),
        copy(wout_cols(ypeer), wout_cols(ypeer), wc_s.at[3], wc_r.at[3], strip=cpeer),
    ]
    mine = rows(z, x)
    tok[0, mine, :] = (grad_ref[...].astype(F32) * scale_ref[...]).astype(BF16)
    pl.semaphore_wait(barrier, 6)
    own_sends(0)
    for c in wy:
        c.start()
    for c in wc[:2]:
        c.start()
    values, inverse = apply_layer_norm(conv_ref[...].astype(F32))
    xhat[...] = values
    inv[...] = inverse
    tok[1, mine, :] = (values * gain_ref[...] + bias_ref[...]).astype(BF16)
    own_sends(1)
    win[pl.ds(pl.multiple_of(strip * shard, shard), shard), :] = win_ref[...]
    wout[:, pl.ds(pl.multiple_of(strip * shard, 128), shard)] = wout_ref[...]
    acc_in[...] = jnp.zeros_like(acc_in)
    acc_out[...] = jnp.zeros_like(acc_out)

    def forward(i):
        b = order(i)
        for h in range(2):
            az_copy(1 + i, h, b, z).wait_recv()
            ax_copy(h, b, x).start()

            @pl.when(zm == 1)
            def _():
                az_copy(1 + i, h, b, unmirror(2 if i == 1 else 0)).start()

    def weights():
        wy[0].wait_recv()
        wc[2].start()
        wy[1].wait_recv()
        wc[3].start()

    forward(1)

    @pl.when(zm == 1)
    def _():
        forward(2)

    weights()

    @pl.when(zm == 0)
    def _():
        forward(2)

    for c in wc:
        c.wait_recv()

    def gx_copy(b):
        return copy(gsend.at[b], gxrecv.at[b], gx_s.at[b], gx_r.at[b], tensor=xpeer)

    def gz_copy(b):
        return copy(zsend.at[b], zrecv.at[z], gz_s.at[b], gz_r.at[z], tensor=2 * b + x)

    def reduce(i):
        b = order(i)
        gx_copy(b).wait_recv()
        joined = gown[b] + gxrecv[b].astype(F32)

        @pl.when(b == z)
        def _():
            total[...] = joined

        @pl.when(b != z)
        def _():
            zsend[b] = joined.astype(BF16)
            gz_copy(b).start()

    hstep = 256
    cstep = 256

    @pl.loop(0, 4)
    def _(i):
        @pl.when((i == 1) & (zm == 1))
        def _():
            forward(3)

        @pl.when((i == 2) & (zm == 0))
        def _():
            forward(3)

        b = order(i)
        for h in range(2):
            ax_copy(h, b, 1 - x).wait_recv()
        pair = pl.ds(pl.multiple_of(b * 2 * count, 2 * count), 2 * count)

        @pl.loop(0, wide // hstep)
        def _(t):
            cols = pl.ds(pl.multiple_of(t * hstep, hstep), hstep)
            pre = jnp.dot(tok[1, pair, :], win[:, cols], preferred_element_type=F32)
            pre = pre + bin_ref[:, cols]
            back = nt(tok[0, pair, :], wout[cols, :])
            cdf = 0.5 * (1.0 + lax.erf(pre * root_half))
            hid[:, cols] = (pre * cdf).astype(BF16)
            slope = cdf + pre * jnp.exp(-0.5 * pre * pre) * density_norm
            bp[:, cols] = (back * slope).astype(BF16)

        def normed_grad(xx, put):
            part = pl.ds(pl.multiple_of(xx * count, count), count)

            @pl.loop(0, channels // cstep)
            def _(t):
                chans = pl.ds(pl.multiple_of(t * cstep, cstep), cstep)
                put(chans, nt(bp[part, :], win[chans, :]))

        def put_send(chans, value):
            gsend[b, :, chans] = value.astype(BF16)

        def put_own(chans, value):
            gown[b, :, chans] = value

        normed_grad(1 - x, put_send)
        gx_copy(b).start()
        normed_grad(x, put_own)

        @pl.loop(0, channels // cstep)
        def _(t):
            chans = pl.ds(pl.multiple_of(t * cstep, cstep), cstep)
            acc_in[chans, :] += tn(tok[1, pair, chans], bp[...])

        @pl.loop(0, wide // hstep)
        def _(t):
            cols = pl.ds(pl.multiple_of(t * hstep, hstep), hstep)
            acc_out[cols, :] += tn(hid[:, cols], tok[0, pair, :])

        @pl.when(i > 0)
        def _():
            reduce(i - 1)

    def in_rows(s):
        return pl.ds(pl.multiple_of(s * shard, shard), shard)

    def out_cols(s):
        return pl.ds(pl.multiple_of(s * shard, 128), shard)

    cc = []
    for k in range(2):
        yy = (1 - y) * (1 - k) + y * k
        s = 2 * yy + 1 - core
        csend_in[k] = acc_in[in_rows(s), :].astype(BF16)
        c = copy(csend_in.at[k], crecv_in.at[k], cs.at[k, 0], cr.at[k, 0], strip=cpeer)
        c.start()
        cc.append(c)
        csend_out[k] = acc_out[:, out_cols(s)].astype(BF16)
        c = copy(csend_out.at[k], crecv_out.at[k], cs.at[k, 1], cr.at[k, 1], strip=cpeer)
        c.start()
        cc.append(c)
    reduce(3)
    cc[0].wait_recv()
    yc = [
        copy(ysend_in, yrecv_in, ys.at[0], yr.at[0], strip=ypeer),
        copy(ysend_out, yrecv_out, ys.at[1], yr.at[1], strip=ypeer),
    ]
    ysend_in[...] = (acc_in[in_rows(ypeer), :] + crecv_in[0].astype(F32)).astype(BF16)
    yc[0].start()
    cc[1].wait_recv()
    ysend_out[...] = (acc_out[:, out_cols(ypeer)] + crecv_out[0].astype(F32)).astype(BF16)
    yc[1].start()
    cc[2].wait_recv()
    gin_ref[...] = acc_in[in_rows(strip), :] + crecv_in[1].astype(F32)
    cc[3].wait_recv()
    gout_ref[...] = acc_out[:, out_cols(strip)] + crecv_out[1].astype(F32)

    def gz_arrival(b):
        return copy(zsend.at[b], zrecv.at[b], gz_s.at[b], gz_r.at[b], tensor=2 * b + x)

    for i in range(1, 4):
        b = order(i)
        gz_arrival(b).wait_recv()
        total[...] += zrecv[b].astype(F32)
    gconv_ref[...] = layer_norm_backward(
        total[...], xhat[...], inv[...], gain_ref[...]
    ).astype(BF16)

    yc[0].wait_recv()
    gin_ref[...] = (gin_ref[...] + yrecv_in[...].astype(F32)) * factor
    yc[1].wait_recv()
    gout_ref[...] = (gout_ref[...] + yrecv_out[...].astype(F32)) * factor

    for c in wy + wc + cc + yc:
        c.wait_send()
    for h in range(2):
        for b in range(4):
            ax_copy(h, b, x).wait_send()
        az_copy(0, h, z, z).wait_send()

        @pl.when(zm == 1)
        def _():
            az_copy(1, h, z, z).wait_send()
            for i in range(1, 4):
                az_copy(1 + i, h, order(i), z).wait_send()

    for b in range(4):
        gx_copy(b).wait_send()
    for i in range(1, 4):
        gz_copy(order(i)).wait_send()


def fast_body(
    conv_out, out_grad, layer_norm_gain, layer_norm_bias, w_in, b_in, w_out, layer_scale, dw_kernel
):
    tile_rows, tile_cols, channels = conv_out.shape
    count = tile_rows * tile_cols
    shard, wide = w_in.shape
    strips, tensors = lax.axis_size("strip"), lax.axis_size("tensor")
    tokens = count * tensors
    factor = 1.0 / math.sqrt(tokens * strips)
    vmem = pl.BlockSpec(memory_space=pltpu.VMEM)
    dma = pltpu.SemaphoreType.DMA
    gconv, gin, gout = pl.pallas_call(
        functools.partial(block_kernel, factor),
        out_shape=(
            jax.ShapeDtypeStruct((count, channels), BF16),
            jax.ShapeDtypeStruct((shard, wide), F32),
            jax.ShapeDtypeStruct((wide, shard), F32),
        ),
        in_specs=[vmem] * 8,
        out_specs=(vmem,) * 3,
        scratch_shapes=[
            pltpu.VMEM((2, tokens, channels), BF16),
            pltpu.VMEM((channels, wide), BF16),
            pltpu.VMEM((wide, channels), BF16),
            pltpu.VMEM((2 * count, wide), BF16),
            pltpu.VMEM((2 * count, wide), BF16),
            pltpu.VMEM((channels, wide), F32),
            pltpu.VMEM((wide, channels), F32),
            pltpu.VMEM((count, channels), F32),
            pltpu.VMEM((count, 1), F32),
            pltpu.VMEM((4, count, channels), F32),
            pltpu.VMEM((4, count, channels), BF16),
            pltpu.VMEM((4, count, channels), BF16),
            pltpu.VMEM((4, count, channels), BF16),
            pltpu.VMEM((4, count, channels), BF16),
            pltpu.VMEM((count, channels), F32),
            pltpu.VMEM((2, shard, wide), BF16),
            pltpu.VMEM((2, wide, shard), BF16),
            pltpu.VMEM((2, shard, wide), BF16),
            pltpu.VMEM((2, wide, shard), BF16),
            pltpu.VMEM((shard, wide), BF16),
            pltpu.VMEM((wide, shard), BF16),
            pltpu.VMEM((shard, wide), BF16),
            pltpu.VMEM((wide, shard), BF16),
            dma((2,)), dma((2,)), dma((4,)), dma((4,)),
            dma((5, 2)), dma((4, 2)), dma((4, 2)), dma((4, 2)),
            dma((4,)), dma((4,)), dma((4,)), dma((4,)),
            dma((2, 2)), dma((2, 2)), dma((2,)), dma((2,)),
        ],
        compiler_params=pltpu.CompilerParams(
            collective_id=0, has_side_effects=True, vmem_limit_bytes=60 * 2**20
        ),
        cost_estimate=pl.CostEstimate(
            flops=10 * tokens * channels * wide,
            bytes_accessed=12 * shard * wide + 6 * count * channels,
            transcendentals=2 * tokens * wide,
        ),
    )(
        conv_out.reshape(count, channels),
        out_grad.reshape(count, channels),
        layer_norm_gain.reshape(1, channels),
        layer_norm_bias.reshape(1, channels),
        w_in,
        b_in.reshape(1, wide),
        w_out,
        layer_scale.reshape(1, channels),
    )
    margin = dw_kernel.shape[0] // 2
    padded = with_halo(
        gconv.reshape(tile_rows, tile_cols, channels), (("strip", 0), ("tensor", 1)), margin
    )
    grad_input = (
        out_grad.astype(F32)
        + transpose_conv(padded.astype(F32), dw_kernel, tile_rows, tile_cols)
    ).astype(BF16)
    return grad_input, gin, gout


def body(
    conv_out, out_grad, layer_norm_gain, layer_norm_bias, w_in, b_in, w_out, layer_scale, dw_kernel
):
    tile_rows, tile_cols, channel_count = conv_out.shape
    local_count = tile_rows * tile_cols
    flattened_rows = conv_out.astype(jnp.float32).reshape(local_count, channel_count)
    centred_input, inverse_deviation = apply_layer_norm(flattened_rows)
    normed_output = (centred_input * layer_norm_gain + layer_norm_bias).astype(jnp.bfloat16)
    upstream = out_grad.astype(jnp.float32)
    scaled_grad = (upstream.reshape(local_count, channel_count) * layer_scale).astype(jnp.bfloat16)
    w_in_part, w_out_part = (
        lax.all_gather(w_in, "strip", axis=0, tiled=True),
        lax.all_gather(w_out, "strip", axis=1, tiled=True),
    )
    normed_all, scaled_all = (
        lax.all_gather(normed_output, "tensor", axis=0, tiled=True),
        lax.all_gather(scaled_grad, "tensor", axis=0, tiled=True),
    )
    pre_act = jnp.dot(normed_all, w_in_part, preferred_element_type=jnp.float32) + b_in
    hidden_act = gelu_value(pre_act).astype(jnp.bfloat16)
    back_act = lax.dot_general(
        scaled_all, w_out_part, (((1,), (1,)), ((), ())), preferred_element_type=jnp.float32
    )
    back_pre = (back_act * gelu_slope(pre_act)).astype(jnp.bfloat16)
    grad_in = lax.dot_general(
        normed_all, back_pre, (((0,), (0,)), ((), ())), preferred_element_type=jnp.float32
    )
    grad_out = lax.dot_general(
        hidden_act, scaled_all, (((0,), (0,)), ((), ())), preferred_element_type=jnp.float32
    )
    normed_gradient = lax.psum_scatter(
        lax.dot_general(
            back_pre, w_in_part, (((1,), (1,)), ((), ())), preferred_element_type=jnp.float32
        ).astype(jnp.bfloat16),
        "tensor",
        scatter_dimension=0,
        tiled=True,
    ).astype(jnp.float32)
    summed_in, summed_out = (
        lax.psum_scatter(grad_in, "strip", scatter_dimension=0, tiled=True),
        lax.psum_scatter(grad_out, "strip", scatter_dimension=1, tiled=True),
    )
    total_tokens = local_count * lax.axis_size("strip") * lax.axis_size("tensor")
    factor = 1.0 / math.sqrt(total_tokens)
    convolution_gradient = (
        layer_norm_backward(normed_gradient, centred_input, inverse_deviation, layer_norm_gain)
        .astype(jnp.bfloat16)
        .reshape(tile_rows, tile_cols, channel_count)
    )
    margin = dw_kernel.shape[0] // 2
    padded = with_halo(convolution_gradient, (("strip", 0), ("tensor", 1)), margin)
    grad_input = (
        upstream + transpose_conv(padded.astype(jnp.float32), dw_kernel, tile_rows, tile_cols)
    ).astype(jnp.bfloat16)
    return (grad_input, summed_in * factor, summed_out * factor)


def solution(mesh):
    small = mesh.shape["strip"] == 4 and mesh.shape["tensor"] == 8
    return jax.shard_map(
        fast_body if small else body,
        mesh=mesh,
        in_specs=(
            P("strip", "tensor", None),
            P("strip", "tensor", None),
            P(),
            P(),
            P("strip", "tensor"),
            P("tensor"),
            P("tensor", "strip"),
            P(),
            P(),
        ),
        out_specs=(P("strip", "tensor", None), P("strip", "tensor"), P("tensor", "strip")),
        check_vma=False,
    )
```

```python
import functools
import math

import jax
import jax.numpy as jnp
from jax import lax
from jax.experimental import pallas as pl
from jax.experimental.pallas import tpu as pltpu
from jax.sharding import PartitionSpec as P

ln_eps = 1e-06
root_half = 0.7071067811865476
density_norm = 0.3989422804014327
MESH = pl.DeviceIdType.MESH
F32 = jnp.float32
BF16 = jnp.bfloat16


def with_halo(block, sides, width):
    for axis, dim in sides:
        count = lax.axis_size(axis)
        forward = [(i, i + 1) for i in range(count - 1)]
        backward = [(target, source) for source, target in forward]
        low = lax.ppermute(
            lax.slice_in_dim(block, block.shape[dim] - width, None, axis=dim), axis, forward
        )
        high = lax.ppermute(lax.slice_in_dim(block, 0, width, axis=dim), axis, backward)
        block = jnp.concatenate([low, block, high], axis=dim)
    return block


def gelu_value(value):
    return 0.5 * value * (1.0 + lax.erf(value * root_half))


def gelu_slope(value):
    return (
        0.5 * (1.0 + lax.erf(value * root_half))
        + value * jnp.exp(-0.5 * value * value) * density_norm
    )


def apply_layer_norm(flattened_rows):
    centre = jnp.mean(flattened_rows, axis=-1, keepdims=True)
    centred = flattened_rows - centre
    spread = jnp.mean(centred * centred, axis=-1, keepdims=True)
    inverse_deviation = lax.rsqrt(spread + ln_eps)
    return (centred * inverse_deviation, inverse_deviation)


def layer_norm_backward(normed_gradient, centred_input, inverse_deviation, layer_norm_gain):
    gain_scaled = normed_gradient * layer_norm_gain
    first_moment = jnp.mean(gain_scaled, axis=-1, keepdims=True)
    second_moment = jnp.mean(gain_scaled * centred_input, axis=-1, keepdims=True)
    return inverse_deviation * (gain_scaled - first_moment - centred_input * second_moment)


def transpose_conv(padded, dw_kernel, image_height, image_breadth):
    taps = dw_kernel.shape[0]
    total = jnp.zeros((image_height, image_breadth, padded.shape[2]), jnp.float32)
    for row_tap in range(taps):
        for col_tap in range(taps):
            start_row = taps - 1 - row_tap
            start_col = taps - 1 - col_tap
            total = (
                total
                + dw_kernel[row_tap, col_tap]
                * padded[
                    start_row : start_row + image_height, start_col : start_col + image_breadth
                ]
            )
    return total


def nt(a, b):
    return lax.dot_general(a, b, (((1,), (1,)), ((), ())), preferred_element_type=F32)


def tn(a, b):
    return lax.dot_general(a, b, (((0,), (0,)), ((), ())), preferred_element_type=F32)


def block_kernel(
    factor, breadth,
    conv_ref, grad_ref, gain_ref, bias_ref, win_ref, bin_ref, wout_ref, scale_ref, dw_ref,
    ginput_ref, gin_ref, gout_ref,
    tok, win, wout, hid, bp, acc_in, acc_out, xhat, inv,
    gown, gsend, gxrecv, zsend, zrecv, total,
    csend_in, csend_out, crecv_in, crecv_out, ysend_in, ysend_out, yrecv_in, yrecv_out,
    wy_s, wy_r, wc_s, wc_r, az_s, az_r, ax_s, ax_r, gx_s, gx_r, gz_s, gz_r,
    vec, bvec, gcb, staged, stage_out, halo_rows, halo_cols, halo_corner, halo_wide, padded,
    cs, cr, ys, yr, hs, hr, ez_s, ez_r,
):
    count, channels = conv_ref.shape
    shard, wide = win_ref.shape
    strip = lax.axis_index("strip")
    tensor = lax.axis_index("tensor")
    y, core = strip // 2, strip % 2
    z, x = tensor // 2, tensor % 2
    up = z // 2
    zm = z * (1 - up) + (3 - z) * up
    ypeer = 2 * (1 - y) + core
    cpeer = 2 * y + 1 - core
    xpeer = 2 * z + 1 - x

    def unmirror(m):
        return m * (1 - up) + (3 - m) * up

    def order(i):
        hi = i // 2
        return unmirror(hi * i + (1 - hi) * (i + zm - 2 * i * zm))

    def copy(src, dst, s, r, **where):
        return pltpu.make_async_remote_copy(
            src_ref=src, dst_ref=dst, send_sem=s, recv_sem=r, device_id=where, device_id_type=MESH
        )

    def rows(b, xx):
        return pl.ds(pl.multiple_of((2 * b + xx) * count, count), count)

    barrier = pltpu.get_barrier_semaphore()
    pl.semaphore_signal(barrier, inc=1, device_id={"strip": ypeer}, device_id_type=MESH)
    pl.semaphore_signal(barrier, inc=1, device_id={"strip": cpeer}, device_id_type=MESH)
    pl.semaphore_signal(barrier, inc=1, device_id={"tensor": xpeer}, device_id_type=MESH)
    for d in range(1, 4):
        other = 2 * ((z + d) % 4) + x
        pl.semaphore_signal(barrier, inc=1, device_id={"tensor": other}, device_id_type=MESH)
    sides = [(a, b) for a in (-1, 0, 1) for b in (-1, 0, 1) if (a, b) != (0, 0)]

    def inside(a, b):
        good = None
        for step, here, size in ((a, strip, 4), (b, tensor, 8)):
            if step:
                one = here > 0 if step < 0 else here < size - 1
                good = one if good is None else good & one
        return good

    for a, b in sides:

        @pl.when(inside(a, b))
        def _():
            pl.semaphore_signal(
                barrier,
                inc=1,
                device_id={"strip": strip + a, "tensor": tensor + b},
                device_id_type=MESH,
            )

    def win_rows(s):
        return win.at[pl.ds(pl.multiple_of(s * shard, shard), shard)]

    def wout_cols(s):
        return wout.at[:, pl.ds(pl.multiple_of(s * shard, 128), shard)]

    def az_copy(k, h, b, dest):
        piece = tok.at[h, rows(b, x)]
        return copy(piece, piece, az_s.at[k, h], az_r.at[b, h], tensor=2 * dest + x)

    def ax_copy(h, b, xx):
        piece = tok.at[h, rows(b, xx)]
        return copy(piece, piece, ax_s.at[b, h], ax_r.at[b, h], tensor=xpeer)

    def own_sends(h):
        az_copy(0, h, z, unmirror(zm + 1)).start()

        @pl.when(zm == 1)
        def _():
            az_copy(1, h, z, unmirror(0)).start()

        ax_copy(h, z, x).start()

    wy = [
        copy(win_ref, win_rows(strip), wy_s.at[0], wy_r.at[0], strip=ypeer),
        copy(wout_ref, wout_cols(strip), wy_s.at[1], wy_r.at[1], strip=ypeer),
    ]
    wc = [
        copy(win_ref, win_rows(strip), wc_s.at[0], wc_r.at[0], strip=cpeer),
        copy(wout_ref, wout_cols(strip), wc_s.at[1], wc_r.at[1], strip=cpeer),
        copy(win_rows(ypeer), win_rows(ypeer), wc_s.at[2], wc_r.at[2], strip=cpeer),
        copy(wout_cols(ypeer), wout_cols(ypeer), wc_s.at[3], wc_r.at[3], strip=cpeer),
    ]
    mine = rows(z, x)
    vec[0:1, :] = gain_ref[...].reshape(1, channels)
    vec[1:2, :] = bias_ref[...].reshape(1, channels)
    vec[2:3, :] = scale_ref[...].reshape(1, channels)
    bvec[...] = bin_ref[...].reshape(1, wide)
    tok[0, mine, :] = (grad_ref[...].astype(F32) * vec[2:3, :]).astype(BF16)
    above = (strip > 0).astype(jnp.int32) + (strip < 3).astype(jnp.int32)
    beside = (tensor > 0).astype(jnp.int32) + (tensor < 7).astype(jnp.int32)
    pl.semaphore_wait(barrier, 6 + above + beside + above * beside)
    own_sends(0)
    for c in wy:
        c.start()
    for c in wc[:2]:
        c.start()
    values, inverse = apply_layer_norm(conv_ref[...].astype(F32))
    xhat[...] = values
    inv[...] = inverse
    tok[1, mine, :] = (values * vec[0:1, :] + vec[1:2, :]).astype(BF16)
    own_sends(1)
    win[pl.ds(pl.multiple_of(strip * shard, shard), shard), :] = win_ref[...]
    wout[:, pl.ds(pl.multiple_of(strip * shard, 128), shard)] = wout_ref[...]
    acc_in[...] = jnp.zeros_like(acc_in)
    acc_out[...] = jnp.zeros_like(acc_out)
    padded[...] = jnp.zeros_like(padded)

    def forward(i):
        b = order(i)
        for h in range(2):
            az_copy(1 + i, h, b, z).wait_recv()
            if h == 0 or i == 2:
                ax_copy(h, b, x).start()
            elif i == 1:

                @pl.when(zm == 0)
                def _():
                    ax_copy(h, b, x).start()

            @pl.when(zm == 1)
            def _():
                az_copy(1 + i, h, b, unmirror(2 if i == 1 else 0)).start()

    def weights():
        wy[0].wait_recv()
        wc[2].start()
        wy[1].wait_recv()
        wc[3].start()

    near, far = unmirror(0), unmirror(3)

    def ez_copy(b, dest):
        piece = tok.at[1, rows(b, 1 - x)]
        return copy(piece, piece, ez_s.at[b], ez_r.at[b], tensor=2 * dest + x)

    forward(1)

    @pl.when(zm == 1)
    def _():
        forward(2)

    @pl.when(zm == 0)
    def _():
        ax_copy(1, z, 1 - x).wait_recv()
        ez_copy(near, unmirror(1)).start()

    weights()

    @pl.when(zm == 1)
    def _():
        ez_copy(near, z).wait_recv()
        ez_copy(near, unmirror(2)).start()

    @pl.when(zm == 0)
    def _():
        forward(2)

    for c in wc:
        c.wait_recv()

    half = channels // 2

    def part_of(c):
        return pl.ds(c * half, half)

    def gx_copy(b, c):
        src, dst = gsend.at[b, :, part_of(c)], gxrecv.at[b, :, part_of(c)]
        return copy(src, dst, gx_s.at[b, c], gx_r.at[b, c], tensor=xpeer)

    def gz_copy(b, c):
        src, dst = zsend.at[b, :, part_of(c)], zrecv.at[z, :, part_of(c)]
        return copy(src, dst, gz_s.at[b, c], gz_r.at[z, c], tensor=2 * b + x)

    def gz_arrival(b, c):
        dst = zrecv.at[b, :, part_of(c)]
        return copy(dst, dst, gz_s.at[b, c], gz_r.at[b, c], tensor=2 * b + x)

    def reduce(i):
        b = order(i)
        for c in range(2):
            part = part_of(c)
            gx_copy(b, c).wait_recv()
            joined = gown[b, :, part] + gxrecv[b, :, part].astype(F32)

            @pl.when(b == z)
            def _():
                total[:, part] = joined

            @pl.when(b != z)
            def _():
                zsend[b, :, part] = joined.astype(BF16)
                gz_copy(b, c).start()

    hstep = 256
    cstep = 256

    def in_rows(s):
        return pl.ds(pl.multiple_of(s * shard, shard), shard)

    def out_cols(s):
        return pl.ds(pl.multiple_of(s * shard, 128), shard)

    def other_core(k):
        return 2 * ((1 - y) * (1 - k) + y * k) + 1 - core

    def core_copy(k, w):
        send, recv = ((csend_in, crecv_in), (csend_out, crecv_out))[w]
        return copy(send.at[k], recv.at[k], cs.at[k, w], cr.at[k, w], strip=cpeer)

    @pl.loop(0, 4)
    def _(i):
        b = order(i)
        ax_copy(0, b, 1 - x).wait_recv()

        @pl.when((i == 2) | (i == 1 - zm))
        def _():
            ax_copy(1, b, 1 - x).wait_recv()

        @pl.when((i == 3) & (zm == 0))
        def _():
            ez_copy(far, z).wait_recv()

        pair = pl.ds(pl.multiple_of(b * 2 * count, 2 * count), 2 * count)

        @pl.loop(0, wide // hstep)
        def _(t):
            cols = pl.ds(pl.multiple_of(t * hstep, hstep), hstep)
            pre = jnp.dot(tok[1, pair, :], win[:, cols], preferred_element_type=F32)
            pre = pre + bvec[:, cols]
            back = nt(tok[0, pair, :], wout[cols, :])
            cdf = 0.5 * (1.0 + lax.erf(pre * root_half))
            hid[:, cols] = (pre * cdf).astype(BF16)
            slope = cdf + pre * jnp.exp(-0.5 * pre * pre) * density_norm
            bp[:, cols] = (back * slope).astype(BF16)

        @pl.when(i == 1 - zm)
        def _():
            forward(3)

        @pl.when((i == 1) & (zm == 1))
        def _():
            ez_copy(far, z).wait_recv()
            ez_copy(far, near).start()

        def normed_grad(xx, c, put):
            part = pl.ds(pl.multiple_of(xx * count, count), count)
            steps = half // cstep

            @pl.loop(c * steps, (c + 1) * steps)
            def _(t):
                chans = pl.ds(pl.multiple_of(t * cstep, cstep), cstep)
                put(chans, nt(bp[part, :], win[chans, :]))

        def put_send(chans, value):
            gsend[b, :, chans] = value.astype(BF16)

        def put_own(chans, value):
            gown[b, :, chans] = value

        for c in range(2):
            normed_grad(1 - x, c, put_send)

            @pl.when(i > 0)
            def _():
                gx_copy(b, c).start()

        @pl.when(i == 3)
        def _():
            for c in range(2):
                gx_copy(z, c).start()

        @pl.loop(0, channels // cstep)
        def _(t):
            chans = pl.ds(pl.multiple_of(t * cstep, cstep), cstep)
            acc_in[chans, :] += tn(tok[1, pair, chans], bp[...])

        @pl.when(i == 3)
        def _():
            for k in range(2):
                csend_in[k] = acc_in[in_rows(other_core(k)), :].astype(BF16)
                core_copy(k, 0).start()

        for c in range(2):
            normed_grad(x, c, put_own)

        @pl.when(i > 1)
        def _():
            reduce(i - 1)

        @pl.loop(0, wide // hstep)
        def _(t):
            cols = pl.ds(pl.multiple_of(t * hstep, hstep), hstep)
            acc_out[cols, :] += tn(hid[:, cols], tok[0, pair, :])

    for k in range(2):
        csend_out[k] = acc_out[:, out_cols(other_core(k))].astype(BF16)
        core_copy(k, 1).start()
    cc = [core_copy(k, w) for k in range(2) for w in range(2)]
    cc[0].wait_recv()
    yc = [
        copy(ysend_in, yrecv_in, ys.at[0], yr.at[0], strip=ypeer),
        copy(ysend_out, yrecv_out, ys.at[1], yr.at[1], strip=ypeer),
    ]
    ysend_in[...] = (acc_in[in_rows(ypeer), :] + crecv_in[0].astype(F32)).astype(BF16)
    yc[0].start()
    cc[1].wait_recv()
    ysend_out[...] = (acc_out[:, out_cols(ypeer)] + crecv_out[0].astype(F32)).astype(BF16)
    yc[1].start()
    reduce(3)
    cc[2].wait_recv()
    gin_ref[...] = acc_in[in_rows(strip), :] + crecv_in[1].astype(F32)
    cc[3].wait_recv()
    gout_ref[...] = acc_out[:, out_cols(strip)] + crecv_out[1].astype(F32)

    reduce(0)
    for i in range(1, 4):
        b = order(i)
        for c in range(2):
            gz_arrival(b, c).wait_recv()
        total[...] += zrecv[b].astype(F32)
    rounded = layer_norm_backward(total[...], xhat[...], inv[...], vec[0:1, :]).astype(BF16)
    gcb[...] = rounded
    total[...] = rounded.astype(F32)

    edge = halo_rows.shape[1]
    quarter = halo_corner.shape[1]

    def side_copy(k, a, b):
        j = sides.index((-a, -b))
        if b == 0:
            src = gcb.at[pl.ds(0 if a < 0 else count - edge, edge)]
            dst = halo_rows.at[0 if -a < 0 else 1]
        elif a == 0:
            src = stage_out.at[0 if b < 0 else 1]
            dst = halo_cols.at[0 if -b < 0 else 1]
        else:
            src = stage_out.at[0 if b < 0 else 1, pl.ds(0 if a < 0 else quarter, quarter)]
            dst = halo_corner.at[(0 if -a < 0 else 2) + (0 if -b < 0 else 1)]
        return copy(src, dst, hs.at[k], hr.at[j], strip=strip + a, tensor=tensor + b)

    def side_arrival(k, a, b):
        if b == 0:
            dst = halo_rows.at[0 if a < 0 else 1]
        elif a == 0:
            dst = halo_cols.at[0 if b < 0 else 1]
        else:
            dst = halo_corner.at[(0 if a < 0 else 2) + (0 if b < 0 else 1)]
        return copy(dst, dst, hs.at[k], hr.at[k], strip=strip + a, tensor=tensor + b)

    def each_side(act, kinds):
        for k, (a, b) in enumerate(sides):
            if (b == 0) == kinds or kinds is None:

                @pl.when(inside(a, b))
                def _():
                    act(k, a, b)

    each_side(lambda k, a, b: side_copy(k, a, b).start(), True)
    height = count // breadth
    for r in range(height):
        staged[0, 4 * r : 4 * r + 4, :] = total[breadth * r : breadth * r + 4, :]
        staged[1, 4 * r : 4 * r + 4, :] = total[breadth * (r + 1) - 4 : breadth * (r + 1), :]
    stage_out[...] = staged[...].astype(BF16)
    each_side(lambda k, a, b: side_copy(k, a, b).start(), False)
    for r in range(height):
        padded[3 + r, 8 : 8 + breadth, :] = total[breadth * r : breadth * (r + 1), :]

    def take(k, a, b):
        side_arrival(k, a, b).wait_recv()
        base = 0 if a < 0 else 3 + height
        left = 4 if b < 0 else 8 + breadth
        if b == 0:
            halo_wide[0:edge, :] = halo_rows[0 if a < 0 else 1].astype(F32)
            for n in range(3):
                padded[base + n, 8 : 8 + breadth, :] = halo_wide[breadth * n : breadth * (n + 1), :]
        elif a == 0:
            halo_wide[0 : 4 * height, :] = halo_cols[0 if b < 0 else 1].astype(F32)
            for r in range(height):
                padded[3 + r, left : left + 4, :] = halo_wide[4 * r : 4 * r + 4, :]
        else:
            corner = halo_corner[(0 if a < 0 else 2) + (0 if b < 0 else 1)]
            halo_wide[0:quarter, :] = corner.astype(F32)
            for n in range(3):
                r = n + 1 if a < 0 else n
                padded[base + n, left : left + 4, :] = halo_wide[4 * r : 4 * r + 4, :]

    each_side(take, None)

    @pl.loop(0, channels // 128)
    def _(t):
        chans = pl.ds(pl.multiple_of(t * 128, 128), 128)
        result = grad_ref[:, chans].astype(F32).reshape(height, breadth, 128)
        for q in range(7):
            moved = padded[:, 11 - q : 11 - q + breadth, chans]
            for p in range(7):
                result = result + dw_ref[p, q : q + 1, chans] * moved[6 - p : 6 - p + height]
        ginput_ref[:, chans] = result.reshape(count, 128).astype(BF16)

    yc[0].wait_recv()
    gin_ref[...] = (gin_ref[...] + yrecv_in[...].astype(F32)) * factor
    yc[1].wait_recv()
    gout_ref[...] = (gout_ref[...] + yrecv_out[...].astype(F32)) * factor

    for c in wy + wc + cc + yc:
        c.wait_send()
    each_side(lambda k, a, b: side_copy(k, a, b).wait_send(), None)
    for i in range(4):
        ax_copy(0, order(i), x).wait_send()
    ax_copy(1, z, x).wait_send()
    ax_copy(1, order(2), x).wait_send()
    ez_copy(near, z).wait_send()
    for h in range(2):
        az_copy(0, h, z, z).wait_send()

    @pl.when(zm == 0)
    def _():
        ax_copy(1, order(1), x).wait_send()

    @pl.when(zm == 1)
    def _():
        ez_copy(far, z).wait_send()
        for h in range(2):
            az_copy(1, h, z, z).wait_send()
            for i in range(1, 4):
                az_copy(1 + i, h, order(i), z).wait_send()

    for c in range(2):
        for b in range(4):
            gx_copy(b, c).wait_send()
        for i in range(1, 4):
            gz_copy(order(i), c).wait_send()


def fast_body(
    conv_out, out_grad, layer_norm_gain, layer_norm_bias, w_in, b_in, w_out, layer_scale, dw_kernel
):
    tile_rows, tile_cols, channels = conv_out.shape
    count = tile_rows * tile_cols
    shard, wide = w_in.shape
    strips, tensors = lax.axis_size("strip"), lax.axis_size("tensor")
    tokens = count * tensors
    factor = 1.0 / math.sqrt(tokens * strips)
    vmem = pl.BlockSpec(memory_space=pltpu.VMEM)
    dma = pltpu.SemaphoreType.DMA
    grad_input, gin, gout = pl.pallas_call(
        functools.partial(block_kernel, factor, tile_cols),
        out_shape=(
            jax.ShapeDtypeStruct((count, channels), BF16),
            jax.ShapeDtypeStruct((shard, wide), F32),
            jax.ShapeDtypeStruct((wide, shard), F32),
        ),
        in_specs=[vmem] * 9,
        out_specs=(vmem,) * 3,
        scratch_shapes=[
            pltpu.VMEM((2, tokens, channels), BF16),
            pltpu.VMEM((channels, wide), BF16),
            pltpu.VMEM((wide, channels), BF16),
            pltpu.VMEM((2 * count, wide), BF16),
            pltpu.VMEM((2 * count, wide), BF16),
            pltpu.VMEM((channels, wide), F32),
            pltpu.VMEM((wide, channels), F32),
            pltpu.VMEM((count, channels), F32),
            pltpu.VMEM((count, 1), F32),
            pltpu.VMEM((4, count, channels), F32),
            pltpu.VMEM((4, count, channels), BF16),
            pltpu.VMEM((4, count, channels), BF16),
            pltpu.VMEM((4, count, channels), BF16),
            pltpu.VMEM((4, count, channels), BF16),
            pltpu.VMEM((count, channels), F32),
            pltpu.VMEM((2, shard, wide), BF16),
            pltpu.VMEM((2, wide, shard), BF16),
            pltpu.VMEM((2, shard, wide), BF16),
            pltpu.VMEM((2, wide, shard), BF16),
            pltpu.VMEM((shard, wide), BF16),
            pltpu.VMEM((wide, shard), BF16),
            pltpu.VMEM((shard, wide), BF16),
            pltpu.VMEM((wide, shard), BF16),
            dma((2,)), dma((2,)), dma((4,)), dma((4,)),
            dma((5, 2)), dma((4, 2)), dma((4, 2)), dma((4, 2)),
            dma((4, 2)), dma((4, 2)), dma((4, 2)), dma((4, 2)),
            pltpu.VMEM((8, channels), F32),
            pltpu.VMEM((1, wide), F32),
            pltpu.VMEM((count, channels), BF16),
            pltpu.VMEM((2, 4 * tile_rows, channels), F32),
            pltpu.VMEM((2, 4 * tile_rows, channels), BF16),
            pltpu.VMEM((2, 3 * tile_cols, channels), BF16),
            pltpu.VMEM((2, 4 * tile_rows, channels), BF16),
            pltpu.VMEM((4, 2 * tile_rows, channels), BF16),
            pltpu.VMEM((3 * tile_cols, channels), F32),
            pltpu.VMEM((tile_rows + 6, tile_cols + 16, channels), F32),
            dma((2, 2)), dma((2, 2)), dma((2,)), dma((2,)), dma((8,)), dma((8,)),
            dma((4,)), dma((4,)),
        ],
        compiler_params=pltpu.CompilerParams(
            collective_id=0, has_side_effects=True, vmem_limit_bytes=60 * 2**20
        ),
        cost_estimate=pl.CostEstimate(
            flops=10 * tokens * channels * wide,
            bytes_accessed=12 * shard * wide + 6 * count * channels,
            transcendentals=2 * tokens * wide,
        ),
    )(
        conv_out.reshape(count, channels),
        out_grad.reshape(count, channels),
        layer_norm_gain,
        layer_norm_bias,
        w_in,
        b_in,
        w_out,
        layer_scale,
        dw_kernel,
    )
    return grad_input.reshape(tile_rows, tile_cols, channels), gin, gout


def body(
    conv_out, out_grad, layer_norm_gain, layer_norm_bias, w_in, b_in, w_out, layer_scale, dw_kernel
):
    tile_rows, tile_cols, channel_count = conv_out.shape
    local_count = tile_rows * tile_cols
    flattened_rows = conv_out.astype(jnp.float32).reshape(local_count, channel_count)
    centred_input, inverse_deviation = apply_layer_norm(flattened_rows)
    normed_output = (centred_input * layer_norm_gain + layer_norm_bias).astype(jnp.bfloat16)
    upstream = out_grad.astype(jnp.float32)
    scaled_grad = (upstream.reshape(local_count, channel_count) * layer_scale).astype(jnp.bfloat16)
    w_in_part, w_out_part = (
        lax.all_gather(w_in, "strip", axis=0, tiled=True),
        lax.all_gather(w_out, "strip", axis=1, tiled=True),
    )
    normed_all, scaled_all = (
        lax.all_gather(normed_output, "tensor", axis=0, tiled=True),
        lax.all_gather(scaled_grad, "tensor", axis=0, tiled=True),
    )
    pre_act = jnp.dot(normed_all, w_in_part, preferred_element_type=jnp.float32) + b_in
    hidden_act = gelu_value(pre_act).astype(jnp.bfloat16)
    back_act = lax.dot_general(
        scaled_all, w_out_part, (((1,), (1,)), ((), ())), preferred_element_type=jnp.float32
    )
    back_pre = (back_act * gelu_slope(pre_act)).astype(jnp.bfloat16)
    grad_in = lax.dot_general(
        normed_all, back_pre, (((0,), (0,)), ((), ())), preferred_element_type=jnp.float32
    )
    grad_out = lax.dot_general(
        hidden_act, scaled_all, (((0,), (0,)), ((), ())), preferred_element_type=jnp.float32
    )
    normed_gradient = lax.psum_scatter(
        lax.dot_general(
            back_pre, w_in_part, (((1,), (1,)), ((), ())), preferred_element_type=jnp.float32
        ).astype(jnp.bfloat16),
        "tensor",
        scatter_dimension=0,
        tiled=True,
    ).astype(jnp.float32)
    summed_in, summed_out = (
        lax.psum_scatter(grad_in, "strip", scatter_dimension=0, tiled=True),
        lax.psum_scatter(grad_out, "strip", scatter_dimension=1, tiled=True),
    )
    total_tokens = local_count * lax.axis_size("strip") * lax.axis_size("tensor")
    factor = 1.0 / math.sqrt(total_tokens)
    convolution_gradient = (
        layer_norm_backward(normed_gradient, centred_input, inverse_deviation, layer_norm_gain)
        .astype(jnp.bfloat16)
        .reshape(tile_rows, tile_cols, channel_count)
    )
    margin = dw_kernel.shape[0] // 2
    padded = with_halo(convolution_gradient, (("strip", 0), ("tensor", 1)), margin)
    grad_input = (
        upstream + transpose_conv(padded.astype(jnp.float32), dw_kernel, tile_rows, tile_cols)
    ).astype(jnp.bfloat16)
    return (grad_input, summed_in * factor, summed_out * factor)


def solution(mesh):
    small = mesh.shape["strip"] == 4 and mesh.shape["tensor"] == 8
    return jax.shard_map(
        fast_body if small else body,
        mesh=mesh,
        in_specs=(
            P("strip", "tensor", None),
            P("strip", "tensor", None),
            P(),
            P(),
            P("strip", "tensor"),
            P("tensor"),
            P("tensor", "strip"),
            P(),
            P(),
        ),
        out_specs=(P("strip", "tensor", None), P("strip", "tensor"), P("tensor", "strip")),
        check_vma=False,
    )
```
